256 devices in a mesh: node: 32 (over y_hi, z, core), local: 8 (over y_lo, x).
Axes of the slice: x: 4, y: 4 (y_hi: 2, y_lo: 2; y = y_hi * 2 + y_lo), z: 8, core: 2. Of those that a mesh axis runs over, the one named last changes fastest.
Arguments:
- hidden_acts: bfloat16 [262144, 1024], P(('node', 'local')), may hold values from -6 to 6
- out_grad: bfloat16 [262144, 4096], P(('node', 'local')), may hold values from -1.5 to 1.5
- live_counts: int32 [32, 8], P('node', 'local'), may hold values from 256 to 1024, as said below
- master: float32 [1024, 4096], P('local', 'node'), may hold values from -2.5 to 2.5
- first: float32 [1024, 4096], P('local', 'node'), may hold values from -15 to 15
- second: float32 [1024, 4096], P('local', 'node'), may hold values from 1 to 100
Outputs:
- new_master: float32 [1024, 4096], P('local', 'node')
- new_first: float32 [1024, 4096], P('local', 'node')
- new_second: float32 [1024, 4096], P('local', 'node')
- weights_next: bfloat16 [1024, 4096], P('local')
The draws below stay inside these ranges and needn't reach their ends.
Inputs may be any that keep to these rules, and one draw needn't show every extreme that they name: `live_counts`: both ends are reached on some device in every draw.
All inputs are finite; a program needn't handle non-finite values.
Results may differ from the reference program's by a relative error of at most 0.001.
Values may be sent and summed in bfloat16 or wider, within the bound.
A program may use at most 128 MiB of HBM per device.

```python
import math
import jax
import jax.numpy as jnp
from jax import lax

D = 4096
FFW = 1024
TOK_DEV = 1024
ADAM_STEP = 10
TOKENS = 262144
N_NODE = 32
N_LOCAL = 8


def draw_live_counts(key, part):
    key = jax.random.fold_in(key, 23)
    key_vals, key_pos = jax.random.split(key)
    total = N_NODE * N_LOCAL
    counts = jax.random.randint(key_vals, (total,), TOK_DEV // 4, TOK_DEV + 1)
    where_top = jax.random.randint(key_pos, (), 0, total)
    counts = counts.at[where_top].set(TOK_DEV)
    counts = counts.at[(where_top + 1) % total].set(TOK_DEV // 4)
    return counts.reshape(N_NODE, N_LOCAL).astype(jnp.int32)


def raised(array, key, source, target, parts, factor):
    owner, partner = [(jnp.arange(array.shape[position]) // (array.shape[position] // parts)).reshape([-1 if axis == position else 1 for axis in range(array.ndim)]) for position in (source, target)]
    chosen = jax.random.permutation(key, parts)[partner]
    strong = (owner == chosen) | (owner == (partner + parts // 2) % parts)
    return jnp.where(strong, factor * array, array)


def steps_of(stream_key, shape, shards, least, high):
    level, own = 1.0, jax.random.fold_in(stream_key, 6)
    for axis_at, parts in shards:
        steps = jnp.exp(jax.random.uniform(jax.random.fold_in(own, axis_at), (parts,), jnp.float32, least / len(shards), high / len(shards)))
        level = level * jnp.repeat(steps, shape[axis_at] // parts).reshape([-1 if axis == axis_at else 1 for axis in range(len(shape))])
    return level


def noise(stream_key, shape, scale, most, shards=(), kind=jnp.bfloat16):
    result = scale * jax.random.normal(stream_key, shape, jnp.float32)
    if shards:
        result = result * steps_of(stream_key, shape, shards, -0.22, 0.18)
    return jnp.clip(result, -most, most).astype(kind)


def heavy_noise(stream_key, dims, width, most, shards, heavy, kind=jnp.bfloat16):
    drawn = width * jax.random.normal(stream_key, dims, jnp.float32)
    if shards:
        drawn = drawn * steps_of(stream_key, dims, shards, -0.22, 0.18)
    return jnp.clip(raised(drawn, jax.random.fold_in(stream_key, 3), *heavy), -most, most).astype(kind)


def setup_inputs(seed: int = 0) -> dict:
    splits = jax.random.split(jax.random.key(seed), 7)
    hidden_acts = noise(splits[0], (TOKENS, FFW), 1.0, 6.0, ((0, 256),))
    out_grad = heavy_noise(splits[1], (TOKENS, D), (2.0 * TOK_DEV ** -0.5), 1.5, ((0, 256),), (0, 1, 256, 6.0))
    live_counts = draw_live_counts(jax.random.fold_in(splits[6], 71), 0)
    master = noise(splits[3], (FFW, D), 0.5, 2.5, ((0, 8), (1, 32)), jnp.float32)
    first = noise(splits[4], (FFW, D), 3.0, 15.0, ((0, 8), (1, 32)), jnp.float32)
    second = jnp.clip(jnp.exp(math.log(100.0) - 4.6051702 * jax.random.uniform(splits[5], (FFW, D), jnp.float32) ** steps_of(splits[5], (FFW, D), ((0, 8), (1, 32)), -0.2, 0.2)), 1.0, 100.0)
    return {"hidden_acts": hidden_acts, "out_grad": out_grad, "live_counts": live_counts, "master": master, "first": first, "second": second}


def reference(hidden_acts, out_grad, live_counts, master, first, second):
    flat_live = live_counts.reshape(-1).astype(jnp.int32)
    blocks_h = hidden_acts.reshape(N_NODE * N_LOCAL, TOK_DEV, FFW)
    blocks_g = out_grad.reshape(N_NODE * N_LOCAL, TOK_DEV, D)

    def accumulate(total, item):
        acts, grads, count = item
        keep = jnp.arange(TOK_DEV, dtype=jnp.int32) < count
        masked = jnp.where(keep[:, None], grads, jnp.zeros_like(grads))
        term = lax.dot_general(acts, masked, (((0,), (0,)), ((), ())), preferred_element_type=jnp.float32)
        return (total + term, None)
    grad, unused = lax.scan(accumulate, jnp.zeros((FFW, D), jnp.float32), (blocks_h, blocks_g, flat_live))
    new_first = 0.9 * first + 0.1 * grad
    new_second = 0.95 * second + 0.05 * grad * grad
    update = new_first / (1.0 - 0.9 ** ADAM_STEP) / (jnp.sqrt(new_second / (1.0 - 0.95 ** ADAM_STEP)) + 1e-08)
    new_master = master - 0.02 * (update + 0.1 * master)
    return (new_master, new_first, new_second, new_master.astype(jnp.bfloat16))
```

```python
import functools

import jax
import jax.numpy as jnp
from jax import lax
from jax.experimental import pallas as pl
from jax.experimental.pallas import tpu as pltpu
from jax.sharding import PartitionSpec as P

ADAM_STEP = 10
MESH = pl.DeviceIdType.MESH
F32, BF16, I16, I32 = jnp.float32, jnp.bfloat16, jnp.int16, jnp.int32
NX, NY, NZ = 4, 4, 8
TOK, FFW, D = 1024, 1024, 4096
BLK = 128
GROUPS = 4
TOP = 32000.0


def send_codes(load, count, out):
    peak = functools.reduce(jnp.maximum, [jnp.abs(load(i)) for i in range(count)])
    power = jnp.ceil(jnp.log2(jnp.maximum(peak, 1e-30)) * 64.0)
    scale = jnp.exp2(power * (-1.0 / 64.0)) * TOP
    out[0] = power.astype(I32).astype(I16)
    for i in range(count):
        out[i + 1] = jnp.round(load(i) * scale).astype(I32).astype(I16)


def unit_of(message):
    return jnp.exp2(message[0].astype(I32).astype(F32) * (1.0 / 64.0)) * (1.0 / TOP)


def decode(message, i, unit):
    return message[i + 1].astype(I32).astype(F32) * unit


def kernel(
    h_hbm, g_hbm, live_ref, master_ref, first_ref, second_ref,
    new_master_ref, new_first_ref, new_second_ref, w_hbm,
    h_buf, ht, gb, s_buf, a1s, a1r, b1s, b1r, a2s, a2r, b2s, b2r, part, keep2, p2s, p2r, p3s, p3r,
    c1s, c1r, rc, c2s, c2r, kc, c3s, c3r, grad, w_buf,
    h_sem, gl_sem, gs_sem, gr_sem, hs_sem, hr_sem,
    one_s, one_r, two_s, two_r, p2_s, p2_r, p3_s, p3_r, c1_s, c1_r, c2_s, c2_r, c3_s, c3_r,
    wz_s, wz_r, wy_s, wy_r, wc_s, wc_r, wo_sem,
):
    node, local = lax.axis_index("node"), lax.axis_index("local")
    core, z, yh = node % 2, (node // 2) % NZ, node // 16
    x, yl = local % 4, local // 4
    y = yh * 2 + yl

    def dev(dx=0, dy=0, dz=0, dc=0):
        tx, ty, tz, tc = (x + dx) % NX, (y + dy) % NY, (z + dz) % NZ, (core + dc) % 2
        return ((ty // 2) * 16 + tz * 2 + tc, (ty % 2) * 4 + tx)

    def remote(src, dst, send, recv, to):
        return pltpu.make_async_remote_copy(
            src_ref=src, dst_ref=dst, send_sem=send, recv_sem=recv, device_id=to, device_id_type=MESH
        )

    def offset(k):
        return 4 + k // 2 - (k % 2) * (1 + 2 * (k // 2))

    def cols(k, half, c):
        block = half * 16 + ((z + offset(k)) % NZ) * 2 + c
        return pl.ds(pl.multiple_of(block * BLK, BLK), BLK)

    def g_local(k, half):
        return pltpu.make_async_copy(
            g_hbm.at[:, cols(k, half, core)], gb.at[k, pl.ds(0, TOK), pl.ds(half * BLK, BLK)], gl_sem.at[k, half]
        )

    def g_remote(k, half):
        return remote(
            g_hbm.at[:, cols(k, half, 1 - core)], gb.at[k, pl.ds(TOK, TOK), pl.ds(half * BLK, BLK)],
            gs_sem.at[k, half], gr_sem.at[k, half], dev(dc=1),
        )

    def h_load(j):
        return pltpu.make_async_copy(h_hbm.at[:, pl.ds(j * 256, 256)], h_buf.at[:, pl.ds(j * 256, 256)], h_sem.at[j])

    def h_remote(j):
        rows = pl.ds(j * 256, 256)
        return remote(
            ht.at[rows, pl.ds(0, TOK)], ht.at[rows, pl.ds(TOK, TOK)], hs_sem.at[j], hr_sem.at[j], dev(dc=1)
        )

    barrier = pltpu.get_barrier_semaphore()
    partners = [dict(dx=1), dict(dx=2), dict(dx=3), dict(dy=1), dict(dy=2), dict(dy=3), dict(dc=1)]
    partners += [dict(dz=i) for i in range(1, NZ)]
    for partner in partners:
        pl.semaphore_signal(barrier, inc=1, device_id=dev(**partner), device_id_type=MESH)
    for j in range(4):
        h_load(j).start()
    for k in range(8):
        for half in range(2):
            g_local(k, half).start()

    live = live_ref[0, 0]

    def turn(j):
        h_load(j).wait()
        alive = lax.broadcasted_iota(I32, (TOK, 256), 0) < live
        block = jnp.where(alive, h_buf[:, pl.ds(j * 256, 256)].astype(F32), 0.0)
        ht[pl.ds(j * 256, 256), pl.ds(0, TOK)] = block.T.astype(BF16)

    turn(0)
    pl.semaphore_wait(barrier, len(partners))
    for k in range(2):
        for half in range(2):
            g_remote(k, half).start()
    h_remote(0).start()
    for j in range(1, 4):
        turn(j)
        h_remote(j).start()
    for k in range(2, 8):
        for half in range(2):
            g_remote(k, half).start()

    def rows_of(block, start):
        return pl.ds(pl.multiple_of(block * BLK + start, 16), 16)

    def a_tile(g, tx, half, i):
        zi, sub, t = i // 6, (i // 3) % 2, i % 3
        return s_buf[2 * g + zi, half, rows_of(sub * 4 + tx, 16 * t), :]

    def b_tile(g, ty, half, i):
        zi, sub, t = i // 6, (i // 3) % 2, i % 3
        return s_buf[2 * g + zi, ty // 2, rows_of((ty % 2) * 4 + 2 * half + sub, 48 + 16 * t), :]

    def one(axis, g, d):
        src, dst = ((a1s, a1r), (b1s, b1r))[axis]
        step = 1 if d == 0 else 3
        to = dev(dx=step) if axis == 0 else dev(dy=step)
        return remote(src.at[g, d], dst.at[g, d], one_s.at[axis, g, d], one_r.at[axis, g, d], to)

    def two(axis, g, d):
        src, dst = ((a2s, a2r), (b2s, b2r))[axis]
        step = 1 if d == 0 else 3
        to = dev(dx=step) if axis == 0 else dev(dy=step)
        return remote(src.at[g, d], dst.at[g, d], two_s.at[axis, g, d], two_r.at[axis, g, d], to)

    tiles = (a_tile, b_tile)
    here = (x, y)

    def first_hop(axis, g):
        src, tile, me = (a1s, b1s)[axis], tiles[axis], here[axis]
        for d in range(2):
            near = (me + (1 if d == 0 else 3)) % 4
            far = (me + 2) % 4

            def load(i, d=d, near=near, far=far):
                return tile(g, far, d, i) if i < 12 else tile(g, near, 1 - d, i - 12)

            send_codes(load, 24, src.at[g, d])
            one(axis, g, d).start()

    def second_hop(axis, g):
        src, got, tile, me = (a2s, b2s)[axis], (a1r, b1r)[axis], tiles[axis], here[axis]
        for d in range(2):
            one(axis, g, d).wait_recv()
            near = (me + (1 if d == 0 else 3)) % 4
            message = got.at[g, d]
            unit = unit_of(message)

            def load(i, d=d, near=near, message=message, unit=unit):
                return tile(g, near, d, i) + decode(message, i, unit)

            send_codes(load, 12, src.at[g, d])
            two(axis, g, d).start()

    def p2(axis, g, j):
        to = dev(dy=j) if axis == 0 else dev(dx=j)
        return remote(p2s.at[axis, g, j - 1], p2r.at[axis, g, j - 1], p2_s.at[axis, g, j - 1], p2_r.at[axis, g, j - 1], to)

    def second_stage(axis, g):
        direct, relayed, tile, me = (a1r, b1r)[axis], (a2r, b2r)[axis], tiles[axis], here[axis]
        for d in range(2):
            two(axis, g, d).wait_recv()
        for half in range(2):
            far, near = relayed.at[g, half], direct.at[g, 1 - half]
            far_unit, near_unit = unit_of(far), unit_of(near)
            for i in range(12):
                zi, sub, t = i // 6, (i // 3) % 2, i % 3
                total = tile(g, me, half, i) + decode(far, i, far_unit) + decode(near, i + 12, near_unit)
                part[axis, 2 * half + sub, zi * 3 + t] = total
        other = here[1 - axis]
        for j in range(1, 4):
            target = (other + j) % 4
            send_codes(lambda i, target=target: part[axis, target, i], 6, p2s.at[axis, g, j - 1])
            p2(axis, g, j).start()
        for i in range(6):
            keep2[g, i // 3, axis * 3 + i % 3] = part[axis, other, i]

    def p3(k):
        return remote(p3s.at[k], p3r.at[k], p3_s.at[k], p3_r.at[k], dev(dz=offset(k)))

    def third_stage(g):
        for axis in range(2):
            units = []
            for j in range(1, 4):
                p2(axis, g, j).wait_recv()
                units.append(unit_of(p2r.at[axis, g, j - 1]))
            for i in range(6):
                total = keep2[g, i // 3, axis * 3 + i % 3]
                for j in range(3):
                    total += decode(p2r.at[axis, g, j], i, units[j])
                keep2[g, i // 3, axis * 3 + i % 3] = total
        for zi in range(2):
            k = 2 * g + zi

            def out(zi=zi, k=k):
                send_codes(lambda i: keep2[g, zi, i], 6, p3s.at[k])
                p3(k).start()

            if zi == 0:
                out()
            else:
                pl.when(g < GROUPS - 1)(out)

    def c_tile(k, half, i):
        return s_buf[k, half, rows_of(i // 2, 96 + 16 * (i % 2)), :]

    def c1(d, s):
        whole = c1s.at[d, s - 1], c1r.at[d, s - 1]
        if s == 4:
            whole = tuple(ref.at[pl.ds(0, 17)] for ref in whole)
        return remote(*whole, c1_s.at[d, s - 1], c1_r.at[d, s - 1], dev(dz=1 if d == 0 else 7))

    def z_index(d, distance):
        return 0 if distance == 4 else 7 - 2 * distance + d

    def z_hop(d, s):
        if s > 1:
            c1(d, s - 1).wait_recv()
            message = c1r.at[d, s - 2]
            unit = unit_of(message)

        def load(i):
            if i < 16:
                value = c_tile(z_index(d, 5 - s), d, i)
            else:
                value = c_tile(z_index(d, 4 - s), 1 - d, i - 16)
            return value + decode(message, i, unit) if s > 1 else value

        send_codes(load, 32 if s < 4 else 16, c1s.at[d, s - 1])
        c1(d, s).start()

    def c2(j):
        return remote(c2s.at[j - 1], c2r.at[j - 1], c2_s.at[j - 1], c2_r.at[j - 1], dev(dx=j))

    def c3(j):
        return remote(c3s.at[j - 1], c3r.at[j - 1], c3_s.at[j - 1], c3_r.at[j - 1], dev(dy=j))

    def c_second():
        for d in range(2):
            c1(d, 4).wait_recv()
        for half in range(2):
            far, near = c1r.at[half, 3], c1r.at[1 - half, 2]
            far_unit, near_unit = unit_of(far), unit_of(near)
            for i in range(16):
                block, t = i // 2, i % 2
                total = c_tile(7, half, i) + decode(far, i, far_unit) + decode(near, i + 16, near_unit)
                rc[block % 4, half * 2 + block // 4, t] = total
        for j in range(1, 4):
            target = (x + j) % 4
            send_codes(lambda i, target=target: rc[target, i // 2, i % 2], 8, c2s.at[j - 1])
            c2(j).start()

    def c_third():
        units = []
        for j in range(1, 4):
            c2(j).wait_recv()
            units.append(unit_of(c2r.at[j - 1]))
        for i in range(8):
            total = rc[x, i // 2, i % 2]
            for j in range(3):
                total += decode(c2r.at[j], i, units[j])
            kc[i // 2, i % 2] = total
        for j in range(1, 4):
            target = (y + j) % 4
            send_codes(lambda i, target=target: kc[target, i], 2, c3s.at[j - 1])
            c3(j).start()

    def c_last():
        units = []
        for j in range(1, 4):
            c3(j).wait_recv()
            units.append(unit_of(c3r.at[j - 1]))
        for i in range(2):
            total = kc[y, i]
            for j in range(3):
                total += decode(c3r.at[j], i, units[j])
            grad[96 + 16 * i : 112 + 16 * i, :] = total

    for j in range(4):
        h_remote(j).wait_recv()

    def multiply(k, carry):
        for half in range(2):
            g_local(k, half).wait()
            g_remote(k, half).wait_recv()
        product = jnp.dot(ht[...], gb[k], preferred_element_type=F32)
        s_buf[k, 0] = product[:, :BLK]
        s_buf[k, 1] = product[:, BLK:]
        return carry

    def round_of(it, carry):
        @pl.when(it < GROUPS)
        def _():
            lax.fori_loop(2 * it, 2 * it + 2, multiply, 0)
            for axis in range(2):
                first_hop(axis, it)

        for s in range(1, 5):
            pl.when(it == s - 1)(functools.partial(z_hop, 0, s))
            pl.when(it == s)(functools.partial(z_hop, 1, s))

        @pl.when((it >= 1) & (it < GROUPS + 1))
        def _():
            for axis in range(2):
                second_hop(axis, it - 1)

        @pl.when((it >= 2) & (it < GROUPS + 2))
        def _():
            for axis in range(2):
                second_stage(axis, it - 2)

        pl.when(it == GROUPS + 1)(c_second)

        @pl.when(it >= 3)
        def _():
            third_stage(it - 3)

        return carry

    lax.fori_loop(0, GROUPS + 3, round_of, 0)
    c_third()
    units = []
    for k in range(7):
        p3(k).wait_recv()
        units.append(unit_of(p3r.at[k]))
    for i in range(6):
        total = keep2[GROUPS - 1, 1, i]
        for k in range(7):
            total += decode(p3r.at[k], i, units[k])
        grad[16 * i : 16 * i + 16, :] = total
    c_last()

    gradient = grad[...]
    new_first = 0.9 * first_ref[...] + 0.1 * gradient
    new_second = 0.95 * second_ref[...] + 0.05 * gradient * gradient
    update = (
        new_first
        / (1.0 - 0.9**ADAM_STEP)
        / (jnp.sqrt(new_second / (1.0 - 0.95**ADAM_STEP)) + 1e-08)
    )
    master = master_ref[...]
    new_master = master - 0.02 * (update + 0.1 * master)
    new_master_ref[...] = new_master
    new_first_ref[...] = new_first
    new_second_ref[...] = new_second

    def w_at(dz=0, dy=0, dc=0):
        block = dev(dz=dz, dy=dy, dc=dc)[0]
        return w_buf.at[:, pl.ds(pl.multiple_of(block * BLK, BLK), BLK)]

    def w_z(j):
        return remote(w_at(), w_at(), wz_s.at[j - 1], wz_r.at[j - 1], dev(dz=j))

    def w_z_got(j):
        return remote(w_at(dz=-j), w_at(dz=-j), wz_s.at[j - 1], wz_r.at[j - 1], dev(dz=j))

    def w_y(j, dy=0):
        return remote(w_at(dz=-j, dy=dy), w_at(dz=-j, dy=dy), wy_s.at[j], wy_r.at[j], dev(dy=2))

    def w_c(j, dy, dc=0):
        at = w_at(dz=-j, dy=dy, dc=dc)
        return remote(at, at, wc_s.at[dy // 2, j], wc_r.at[dy // 2, j], dev(dc=1))

    w_at()[...] = new_master.astype(BF16)
    for j in (4, 3, 5, 2, 6, 1, 7):
        w_z(j).start()
    w_y(0).start()
    w_c(0, 0).start()
    for j in (1, 7, 2, 6, 3, 5, 4):
        w_z_got(j).wait_recv()
        w_y(j).start()
        w_c(j, 0).start()
    for j in (0, 1, 7, 2, 6, 3, 5, 4):
        w_y(j, dy=2).wait_recv()
        w_c(j, 2).start()
    for j in range(8):
        for dy in (0, 2):
            w_c(j, dy, dc=1).wait_recv()
    out = pltpu.make_async_copy(w_buf, w_hbm, wo_sem)
    out.start()

    for j in range(4):
        h_remote(j).wait_send()
    for k in range(8):
        for half in range(2):
            g_remote(k, half).wait_send()
    for axis in range(2):
        for g in range(GROUPS):
            for d in range(2):
                one(axis, g, d).wait_send()
                two(axis, g, d).wait_send()
            for j in range(1, 4):
                p2(axis, g, j).wait_send()
    for k in range(7):
        p3(k).wait_send()
    for d in range(2):
        for s in range(1, 5):
            c1(d, s).wait_send()
    for j in range(1, 4):
        c2(j).wait_send()
        c3(j).wait_send()
    for j in range(1, 8):
        w_z(j).wait_send()
    for j in range(8):
        w_y(j).wait_send()
        for dy in (0, 2):
            w_c(j, dy).wait_send()
    out.wait()


def body(hidden_acts, out_grad, live_counts, master, first, second):
    vmem, smem, anywhere = (pl.BlockSpec(memory_space=m) for m in (pltpu.VMEM, pltpu.SMEM, pl.ANY))
    dma = pltpu.SemaphoreType.DMA

    def tiles(*shape, kind=I16):
        return pltpu.VMEM((*shape, 16, BLK), kind)

    block = jax.ShapeDtypeStruct((BLK, BLK), F32)
    return pl.pallas_call(
        kernel,
        out_shape=(block, block, block, jax.ShapeDtypeStruct((BLK, D), BF16)),
        in_specs=[anywhere, anywhere, smem, vmem, vmem, vmem],
        out_specs=(vmem, vmem, vmem, anywhere),
        scratch_shapes=[
            pltpu.VMEM((TOK, FFW), BF16),
            pltpu.VMEM((FFW, 2 * TOK), BF16),
            pltpu.VMEM((8, 2 * TOK, 256), BF16),
            pltpu.VMEM((8, 2, FFW, BLK), F32),
            tiles(4, 2, 25), tiles(4, 2, 25), tiles(4, 2, 25), tiles(4, 2, 25),
            tiles(4, 2, 13), tiles(4, 2, 13), tiles(4, 2, 13), tiles(4, 2, 13),
            tiles(2, 4, 6, kind=F32), tiles(4, 2, 6, kind=F32),
            tiles(2, 4, 3, 7), tiles(2, 4, 3, 7),
            tiles(7, 7), tiles(7, 7),
            tiles(2, 4, 33), tiles(2, 4, 33), tiles(4, 4, 2, kind=F32),
            tiles(3, 9), tiles(3, 9), tiles(4, 2, kind=F32),
            tiles(3, 3), tiles(3, 3),
            pltpu.VMEM((BLK, BLK), F32),
            pltpu.VMEM((BLK, D), BF16),
            dma((4,)), dma((8, 2)), dma((8, 2)), dma((8, 2)), dma((4,)), dma((4,)),
            dma((2, 4, 2)), dma((2, 4, 2)), dma((2, 4, 2)), dma((2, 4, 2)),
            dma((2, 4, 3)), dma((2, 4, 3)), dma((7,)), dma((7,)),
            dma((2, 4)), dma((2, 4)), dma((3,)), dma((3,)), dma((3,)), dma((3,)),
            dma((7,)), dma((7,)), dma((8,)), dma((8,)), dma((2, 8)), dma((2, 8)), dma(()),
        ],
        compiler_params=pltpu.CompilerParams(
            collective_id=0, has_side_effects=True, vmem_limit_bytes=60 * 1024 * 1024
        ),
        cost_estimate=pl.CostEstimate(
            flops=2 * TOK * FFW * D, bytes_accessed=12 * 1024 * 1024, transcendentals=0
        ),
        name="grad_update",
    )(hidden_acts, out_grad, live_counts, master, first, second)


def solution(mesh):
    in_specs = (
        P(("node", "local"), None),
        P(("node", "local"), None),
        P("node", "local"),
        P("local", "node"),
        P("local", "node"),
        P("local", "node"),
    )
    out_specs = (P("local", "node"), P("local", "node"), P("local", "node"), P("local", None))
    return jax.shard_map(body, mesh=mesh, in_specs=in_specs, out_specs=out_specs, check_vma=False)
```

```python
import functools

import jax
import jax.numpy as jnp
from jax import lax
from jax.experimental import pallas as pl
from jax.experimental.pallas import tpu as pltpu
from jax.sharding import PartitionSpec as P

ADAM_STEP = 10
MESH = pl.DeviceIdType.MESH
F32, BF16, I16, I32 = jnp.float32, jnp.bfloat16, jnp.int16, jnp.int32
NX, NY, NZ = 4, 4, 8
TOK, FFW, D = 1024, 1024, 4096
BLK = 128
GROUPS = 4
TOP = 32000.0
Z_AT = ((2, 3), (5, 6), (8, 8), (10, 10))


def send_codes(load, count, out):
    peak = functools.reduce(jnp.maximum, [jnp.abs(load(i)) for i in range(count)])
    power = jnp.ceil(jnp.log2(jnp.maximum(peak, 1e-30)) * 64.0)
    scale = jnp.exp2(power * (-1.0 / 64.0)) * TOP
    out[0] = power.astype(I32).astype(I16)
    for i in range(count):
        out[i + 1] = jnp.round(load(i) * scale).astype(I32).astype(I16)


def unit_of(message):
    return jnp.exp2(message[0].astype(I32).astype(F32) * (1.0 / 64.0)) * (1.0 / TOP)


def decode(message, i, unit):
    return message[i + 1].astype(I32).astype(F32) * unit


def adamw(grad, master, first, second):
    new_first = 0.9 * first + 0.1 * grad
    new_second = 0.95 * second + 0.05 * grad * grad
    update = (
        new_first
        / (1.0 - 0.9**ADAM_STEP)
        / (jnp.sqrt(new_second / (1.0 - 0.95**ADAM_STEP)) + 1e-08)
    )
    return master - 0.02 * (update + 0.1 * master), new_first, new_second


def kernel(
    h_hbm, g_hbm, live_ref, master_ref, first_ref, second_ref,
    new_master_ref, new_first_ref, new_second_ref, w_ref,
    h_buf, ht, gb, xs, xr, s_buf, m1s, m1r, m2s, m2r, part, keep2, p2s, p2r, p3s, p3r,
    c1s, c1r, c4s, c4r, rc, c2s, c2r, kc, c3s, c3r, grad, w_buf,
    h_sem, gl_sem, xs_sem, xr_sem, one_s, one_r, two_s, two_r, p2_s, p2_r, p3_s, p3_r,
    c1_s, c1_r, c4_s, c2_s, c2_r, c3_s, c3_r, wz_s, wz_r, wy_s, wy_r, wc_s, wc_r,
):
    node, local = lax.axis_index("node"), lax.axis_index("local")
    core, z, yh = node % 2, (node // 2) % NZ, node // 16
    x, yl = local % 4, local // 4
    y = yh * 2 + yl

    def dev(dx=0, dy=0, dz=0, dc=0):
        tx, ty, tz, tc = (x + dx) % NX, (y + dy) % NY, (z + dz) % NZ, (core + dc) % 2
        return ((ty // 2) * 16 + tz * 2 + tc, (ty % 2) * 4 + tx)

    def remote(src, dst, send, recv, to):
        return pltpu.make_async_remote_copy(
            src_ref=src, dst_ref=dst, send_sem=send, recv_sem=recv, device_id=to, device_id_type=MESH
        )

    def offset(k):
        return 4 + k // 2 - (k % 2) * (1 + 2 * (k // 2))

    def cols(k, half, c):
        block = half * 16 + ((z + offset(k)) % NZ) * 2 + c
        return pl.ds(pl.multiple_of(block * BLK, BLK), BLK)

    def g_local(k, whose, half):
        return pltpu.make_async_copy(
            g_hbm.at[:, cols(k, half, (core + whose) % 2)],
            gb.at[k, :, pl.ds((2 * whose + half) * BLK, BLK)],
            gl_sem.at[k],
        )

    def swap(k):
        return remote(xs.at[k], xr.at[k], xs_sem, xr_sem.at[k], dev(dc=1))

    def wait_for(ref, sem):
        pltpu.make_async_copy(ref, ref, sem).wait()

    def h_load(j):
        return pltpu.make_async_copy(h_hbm.at[:, pl.ds(j * 256, 256)], h_buf.at[:, pl.ds(j * 256, 256)], h_sem.at[j])

    barrier = pltpu.get_barrier_semaphore()
    partners = [dict(dx=1), dict(dx=2), dict(dx=3), dict(dy=1), dict(dy=2), dict(dy=3), dict(dc=1)]
    partners += [dict(dz=i) for i in range(1, NZ)]
    for partner in partners:
        pl.semaphore_signal(barrier, inc=1, device_id=dev(**partner), device_id_type=MESH)
    for j in range(4):
        h_load(j).start()
    for k in range(8):
        for whose in range(2):
            for half in range(2):
                g_local(k, whose, half).start()

    live = live_ref[0, 0]

    def turn(j):
        h_load(j).wait()
        alive = lax.broadcasted_iota(I32, (TOK, 256), 0) < live
        block = jnp.where(alive, h_buf[:, pl.ds(j * 256, 256)].astype(F32), 0.0)
        ht[pl.ds(j * 256, 256), :] = block.T.astype(BF16)

    for j in range(4):
        turn(j)
    pl.semaphore_wait(barrier, len(partners))

    def rows_of(block, start, count=16):
        return pl.ds(pl.multiple_of(block * BLK + start, 16), count)

    def a_tile(k, tx, half, i):
        return s_buf[k, half, rows_of((i // 3) * 4 + tx, 16 * (i % 3)), :]

    def b_tile(k, ty, half, i):
        return s_buf[k, ty // 2, rows_of((ty % 2) * 4 + 2 * half + i // 3, 48 + 16 * (i % 3)), :]

    def hop(stage, axis, k, d):
        src, dst, send, recv = ((m1s, m1r, one_s, one_r.at[k]), (m2s, m2r, two_s, two_r.at[k // 2]))[stage]
        step = 1 if d == 0 else 3
        to = dev(dx=step) if axis == 0 else dev(dy=step)
        return remote(src.at[k, axis, d], dst.at[k, axis, d], send, recv, to)

    tiles = (a_tile, b_tile)
    here = (x, y)

    def first_hop(k):
        for axis in range(2):
            tile, me = tiles[axis], here[axis]
            for d in range(2):
                near = (me + (1 if d == 0 else 3)) % 4
                far = (me + 2) % 4

                def load(i, d=d, near=near, far=far, tile=tile):
                    return tile(k, far, d, i) if i < 6 else tile(k, near, 1 - d, i - 6)

                send_codes(load, 12, m1s.at[k, axis, d])
                hop(0, axis, k, d).start()

    def second_hop(k):
        wait_for(m1r.at[k], one_r.at[k])
        for axis in range(2):
            tile, me = tiles[axis], here[axis]
            for d in range(2):
                near = (me + (1 if d == 0 else 3)) % 4
                message = m1r.at[k, axis, d]
                unit = unit_of(message)

                def load(i, d=d, near=near, message=message, unit=unit, tile=tile):
                    return tile(k, near, d, i) + decode(message, i, unit)

                send_codes(load, 6, m2s.at[k, axis, d])
                hop(1, axis, k, d).start()

    def p2(axis, g, j):
        to = dev(dy=j) if axis == 0 else dev(dx=j)
        return remote(p2s.at[g, axis, j - 1], p2r.at[g, axis, j - 1], p2_s, p2_r.at[g], to)

    def second_stage(g):
        wait_for(m2r.at[pl.ds(2 * g, 2)], two_r.at[g])
        for axis in range(2):
            tile, me = tiles[axis], here[axis]
            for zi in range(2):
                k = 2 * g + zi
                for half in range(2):
                    far, near = m2r.at[k, axis, half], m1r.at[k, axis, 1 - half]
                    far_unit, near_unit = unit_of(far), unit_of(near)
                    for i in range(6):
                        total = tile(k, me, half, i) + decode(far, i, far_unit) + decode(near, i + 6, near_unit)
                        part[axis, 2 * half + i // 3, zi * 3 + i % 3] = total
            other = here[1 - axis]
            for j in range(1, 4):
                target = (other + j) % 4
                send_codes(lambda i, axis=axis, target=target: part[axis, target, i], 6, p2s.at[g, axis, j - 1])
                p2(axis, g, j).start()
            for i in range(6):
                keep2[g, i // 3, axis * 3 + i % 3] = part[axis, other, i]

    def p3(k):
        return remote(p3s.at[k], p3r.at[k], p3_s, p3_r, dev(dz=offset(k)))

    def third_stage(g):
        wait_for(p2r.at[g], p2_r.at[g])
        for axis in range(2):
            units = [unit_of(p2r.at[g, axis, j]) for j in range(3)]
            for i in range(6):
                total = keep2[g, i // 3, axis * 3 + i % 3]
                for j in range(3):
                    total += decode(p2r.at[g, axis, j], i, units[j])
                keep2[g, i // 3, axis * 3 + i % 3] = total
        for zi in range(2):
            k = 2 * g + zi

            def out(zi=zi, k=k):
                send_codes(lambda i: keep2[g, zi, i], 6, p3s.at[k])
                p3(k).start()

            if zi == 0:
                out()
            else:
                pl.when(g < GROUPS - 1)(out)

    def c_tile(k, half, i):
        return s_buf[k, half, rows_of(i // 2, 96 + 16 * (i % 2)), :]

    def c1(d, s):
        src, dst, send = (c1s.at[d, s - 1], c1r.at[d, s - 1], c1_s) if s < 4 else (c4s.at[d], c4r.at[d], c4_s)
        return remote(src, dst, send, c1_r.at[d, s - 1], dev(dz=1 if d == 0 else 7))

    def z_index(d, distance):
        return 0 if distance == 4 else 7 - 2 * distance + d

    def z_hop(d, s):
        if s > 1:
            c1(d, s - 1).wait_recv()
            message = c1r.at[d, s - 2]
            unit = unit_of(message)

        def load(i):
            if i < 16:
                value = c_tile(z_index(d, 5 - s), d, i)
            else:
                value = c_tile(z_index(d, 4 - s), 1 - d, i - 16)
            return value + decode(message, i, unit) if s > 1 else value

        send_codes(load, 32 if s < 4 else 16, c1s.at[d, s - 1] if s < 4 else c4s.at[d])
        c1(d, s).start()

    def c2(j):
        return remote(c2s.at[j - 1], c2r.at[j - 1], c2_s, c2_r, dev(dx=j))

    def c3(j):
        return remote(c3s.at[j - 1], c3r.at[j - 1], c3_s, c3_r, dev(dy=j))

    def c_second():
        for d in range(2):
            c1(d, 4).wait_recv()
        for half in range(2):
            far, near = c4r.at[half], c1r.at[1 - half, 2]
            far_unit, near_unit = unit_of(far), unit_of(near)
            for i in range(16):
                block, t = i // 2, i % 2
                total = c_tile(7, half, i) + decode(far, i, far_unit) + decode(near, i + 16, near_unit)
                rc[block % 4, half * 2 + block // 4, t] = total
        for j in range(1, 4):
            target = (x + j) % 4
            send_codes(lambda i, target=target: rc[target, i // 2, i % 2], 8, c2s.at[j - 1])
            c2(j).start()

    def c_third():
        wait_for(c2r, c2_r)
        units = [unit_of(c2r.at[j]) for j in range(3)]
        for i in range(8):
            total = rc[x, i // 2, i % 2]
            for j in range(3):
                total += decode(c2r.at[j], i, units[j])
            kc[i // 2, i % 2] = total
        for j in range(1, 4):
            target = (y + j) % 4
            send_codes(lambda i, target=target: kc[target, i], 2, c3s.at[j - 1])
            c3(j).start()

    def c_last():
        wait_for(c3r, c3_r)
        units = [unit_of(c3r.at[j]) for j in range(3)]
        for i in range(2):
            total = kc[y, i]
            for j in range(3):
                total += decode(c3r.at[j], i, units[j])
            grad[96 + 16 * i : 112 + 16 * i, :] = total

    def multiply(k):
        wait_for(gb.at[k], gl_sem.at[k])
        product = jnp.dot(ht[...], gb[k], preferred_element_type=F32)
        for half in range(2):
            s_buf[k, half] = product[:, half * BLK : half * BLK + BLK]
            xs[k, half] = product[:, (2 + half) * BLK : (3 + half) * BLK]
        swap(k).start()

    def add_core(k):
        swap(k).wait_recv()

        def add(block, carry):
            rows = rows_of(block, 0, BLK)
            for half in range(2):
                s_buf[k, half, rows, :] += xr[k, half, rows, :]
            return carry

        lax.fori_loop(0, 8, add, 0)

    def round_of(it, carry):
        pl.when(it < 8)(lambda: multiply(it))

        @pl.when((it >= 1) & (it < 9))
        def _():
            add_core(it - 1)
            first_hop(it - 1)

        for s, when in enumerate(Z_AT, 1):
            for d in range(2):
                pl.when(it == when[d])(functools.partial(z_hop, d, s))

        pl.when((it >= 3) & (it < 11))(lambda: second_hop(it - 3))
        pl.when((it >= 6) & (it < 13) & (it % 2 == 0))(lambda: second_stage((it - 6) // 2))
        pl.when(it == 12)(c_second)
        pl.when((it >= 8) & (it % 2 == 0))(lambda: third_stage((it - 8) // 2))
        return carry

    lax.fori_loop(0, 15, round_of, 0)
    c_third()
    wait_for(p3r, p3_r)
    units = [unit_of(p3r.at[k]) for k in range(7)]
    for i in range(6):
        total = keep2[GROUPS - 1, 1, i]
        for k in range(7):
            total += decode(p3r.at[k], i, units[k])
        grad[16 * i : 16 * i + 16, :] = total
    c_last()

    new_master, new_first, new_second = adamw(grad[...], master_ref[...], first_ref[...], second_ref[...])

    def w_at(dz=0, dy=0, dc=0):
        block = dev(dz=dz, dy=dy, dc=dc)[0]
        return w_buf.at[:, pl.ds(pl.multiple_of(block * BLK, BLK), BLK)]

    z_sends = ((0, 1, 0, BLK), (0, 7, 0, BLK), (0, 2, 0, BLK), (0, 6, 0, BLK), (6, 1, 0, BLK), (2, 7, 0, BLK), (6, 2, 0, 64), (2, 6, 64, 64))

    def w_z(i, got=False):
        block, to, start, count = z_sends[i]
        at = w_at(dz=block - to if got else block).at[pl.ds(start, count)]
        return remote(at, at, wz_s, wz_r.at[min(i, 6)], dev(dz=to))

    def w_y(j, dy=0):
        return remote(w_at(dz=-j, dy=dy), w_at(dz=-j, dy=dy), wy_s, wy_r.at[j], dev(dy=2))

    def w_c(j, dy):
        at = w_at(dz=-j, dy=dy)
        return remote(at, at, wc_s, wc_r, dev(dc=1))

    w_at()[...] = new_master.astype(BF16)
    def spread(j):
        w_y(j).start()
        w_c(j, 0).start()

    for i in (2, 3, 0, 1):
        w_z(i).start()
    spread(0)
    new_master_ref[...] = new_master
    new_first_ref[...] = new_first
    new_second_ref[...] = new_second
    w_z(2, got=True).wait_recv()
    w_z(4).start()
    w_z(6).start()
    w_z(3, got=True).wait_recv()
    w_z(5).start()
    w_z(7).start()
    for i, j in ((0, 1), (1, 7)):
        w_z(i, got=True).wait_recv()
        spread(j)
    spread(2)
    spread(6)
    for i, j in ((4, 3), (5, 5)):
        w_z(i, got=True).wait_recv()
        spread(j)
    wait_for(w_at(dz=4), wz_r.at[6])
    spread(4)
    for j in (0, 1, 7, 2, 6, 3, 5, 4):
        w_y(j, dy=2).wait_recv()
        w_c(j, 2).start()
    def blocks(count):
        return w_buf.at[:, pl.ds(0, count * BLK)]

    wait_for(blocks(16), wc_r)
    w_ref[...] = w_buf[...]

    for ref, sem in (
        (xs, xs_sem), (m1s, one_s), (m2s, two_s), (p2s, p2_s), (p3s, p3_s), (c1s, c1_s), (c4s, c4_s), (c2s, c2_s), (c3s, c3_s),
        (blocks(7), wz_s), (blocks(8), wy_s), (blocks(16), wc_s),
    ):
        wait_for(ref, sem)


def body(hidden_acts, out_grad, live_counts, master, first, second):
    vmem, smem, anywhere = (pl.BlockSpec(memory_space=m) for m in (pltpu.VMEM, pltpu.SMEM, pl.ANY))
    dma = pltpu.SemaphoreType.DMA

    def tiles(*shape, kind=I16):
        return pltpu.VMEM((*shape, 16, BLK), kind)

    block = pltpu.VMEM((BLK, BLK), F32)
    return pl.pallas_call(
        kernel,
        out_shape=(block, block, block, pltpu.VMEM((BLK, D), BF16)),
        in_specs=[anywhere, anywhere, smem, vmem, vmem, vmem],
        out_specs=(vmem, vmem, vmem, vmem),
        scratch_shapes=[
            pltpu.VMEM((TOK, FFW), BF16),
            pltpu.VMEM((FFW, TOK), BF16),
            pltpu.VMEM((8, TOK, 4 * BLK), BF16),
            pltpu.VMEM((8, 2, FFW, BLK), F32), pltpu.VMEM((8, 2, FFW, BLK), F32), pltpu.VMEM((8, 2, FFW, BLK), F32),
            tiles(8, 2, 2, 13), tiles(8, 2, 2, 13), tiles(8, 2, 2, 7), tiles(8, 2, 2, 7),
            tiles(2, 4, 6, kind=F32), tiles(4, 2, 6, kind=F32),
            tiles(4, 2, 3, 7), tiles(4, 2, 3, 7), tiles(7, 7), tiles(7, 7),
            tiles(2, 3, 33), tiles(2, 3, 33), tiles(2, 17), tiles(2, 17), tiles(4, 4, 2, kind=F32),
            tiles(3, 9), tiles(3, 9), tiles(4, 2, kind=F32), tiles(3, 3), tiles(3, 3),
            pltpu.VMEM((BLK, BLK), F32),
            pltpu.VMEM((BLK, D), BF16),
            dma((4,)), dma((8,)), dma(()), dma((8,)), dma(()), dma((8,)), dma(()), dma((4,)), dma(()), dma((4,)), dma(()), dma(()),
            dma(()), dma((2, 4)), dma(()), dma(()), dma(()), dma(()), dma(()),
            dma(()), dma((7,)), dma(()), dma((8,)), dma(()), dma(()),
        ],
        compiler_params=pltpu.CompilerParams(
            collective_id=0, has_side_effects=True, vmem_limit_bytes=60 * 1024 * 1024
        ),
        cost_estimate=pl.CostEstimate(
            flops=2 * TOK * FFW * D, bytes_accessed=12 * 1024 * 1024, transcendentals=0
        ),
        name="grad_update",
    )(hidden_acts, out_grad, live_counts, master, first, second)

def solution(mesh):
    in_specs = (
        P(("node", "local"), None),
        P(("node", "local"), None),
        P("node", "local"),
        P("local", "node"),
        P("local", "node"),
        P("local", "node"),
    )
    out_specs = (P("local", "node"), P("local", "node"), P("local", "node"), P("local", None))
    return jax.shard_map(body, mesh=mesh, in_specs=in_specs, out_specs=out_specs, check_vma=False)
```

```python
import functools

import jax
import jax.numpy as jnp
from jax import lax
from jax.experimental import pallas as pl
from jax.experimental.pallas import tpu as pltpu
from jax.sharding import PartitionSpec as P

ADAM_STEP = 10
MESH = pl.DeviceIdType.MESH
F32, BF16, I16, I32 = jnp.float32, jnp.bfloat16, jnp.int16, jnp.int32
NX, NY, NZ = 4, 4, 8
TOK, FFW, D = 1024, 1024, 4096
BLK = 128
GROUPS = 4
TOP = 32000.0
Z_AT = ((2, 3), (4, 5), (6, 7), (8, 9))
C_AT = (11, 13)
LAG = (3, 6, 8)


def send_codes(load, count, out):
    peak = functools.reduce(jnp.maximum, [jnp.abs(load(i)) for i in range(count)])
    power = jnp.ceil(jnp.log2(jnp.maximum(peak, 1e-30)) * 64.0)
    scale = jnp.exp2(power * (-1.0 / 64.0)) * TOP
    out[0] = power.astype(I32).astype(I16)
    for i in range(count):
        out[i + 1] = jnp.round(load(i) * scale).astype(I32).astype(I16)


def unit_of(message):
    return jnp.exp2(message[0].astype(I32).astype(F32) * (1.0 / 64.0)) * (1.0 / TOP)


def decode(message, i, unit):
    return message[i + 1].astype(I32).astype(F32) * unit


def adamw(grad, master, first, second):
    new_first = 0.9 * first + 0.1 * grad
    new_second = 0.95 * second + 0.05 * grad * grad
    update = (
        new_first
        / (1.0 - 0.9**ADAM_STEP)
        / (jnp.sqrt(new_second / (1.0 - 0.95**ADAM_STEP)) + 1e-08)
    )
    return master - 0.02 * (update + 0.1 * master), new_first, new_second


def hand_out(*refs):
    sources, targets, sem = refs[:4], refs[4:8], refs[8]
    copies = [pltpu.make_async_copy(a, b, sem.at[i]) for i, (a, b) in enumerate(zip(sources, targets))]
    for copy in copies:
        copy.start()
    for copy in copies:
        copy.wait()


def kernel(
    h_hbm, g_hbm, live_ref, master_ref, first_ref, second_ref,
    new_master_ref, new_first_ref, new_second_ref, w_ref,
    h_buf, ht, gb, xs, xr, s_buf, m1s, m1r, m2s, m2r, part, keep2, p2s, p2r, p3s, p3r,
    c1s, c1r, rc, c2s, c2r, kc, c3s, c3r, grad, w_buf,
    h_sem, gl_sem, xs_sem, xr_sem, one_s, one_r, two_s, two_r, p2_s, p2_r, p3_s, p3_r,
    c1_s, c1_r, c2_s, c2_r, c3_s, c3_r, wz_s, wz_r, wy_s, wy_r, wc_s, wc_r,
):
    node, local = lax.axis_index("node"), lax.axis_index("local")
    core, z, yh = lax.rem(node, 2), lax.rem(lax.div(node, 2), NZ), lax.div(node, 16)
    x, yl = lax.rem(local, 4), lax.div(local, 4)
    y = yh * 2 + yl

    xs_at = [lax.rem(x + i, NX) for i in range(NX)]
    ys_at = [lax.rem(y + i, NY) for i in range(NY)]
    zs_at = [lax.rem(z + i, NZ) for i in range(NZ)]
    to_x = [(node, yl * 4 + at) for at in xs_at]
    to_y = [(lax.div(at, 2) * 16 + lax.rem(node, 16), lax.rem(at, 2) * 4 + x) for at in ys_at]
    z_nodes = [[half * 16 + at * 2 + core for at in zs_at] for half in (yh, 1 - yh)]
    to_z = [(at, local) for at in z_nodes[0]]
    to_core = (node + 1 - 2 * core, local)

    def remote(src, dst, send, recv, to):
        return pltpu.make_async_remote_copy(
            src_ref=src, dst_ref=dst, send_sem=send, recv_sem=recv, device_id=to, device_id_type=MESH
        )

    def cols(k, half, whose):
        away = 4 + k // 2 if k % 2 == 0 else 3 - k // 2
        block = half * 16 + zs_at[away] * 2 + (1 - core if whose else core)
        return pl.ds(pl.multiple_of(block * BLK, BLK), BLK)

    def g_local(k, whose, half):
        return pltpu.make_async_copy(
            g_hbm.at[:, cols(k, half, whose)],
            gb.at[k, :, pl.ds((2 * whose + half) * BLK, BLK)],
            gl_sem.at[k],
        )

    def swap(k):
        return remote(xs.at[k], xr.at[k], xs_sem, xr_sem.at[k], to_core)

    def wait_for(ref, sem):
        pltpu.make_async_copy(ref, ref, sem).wait()

    def h_load(j):
        return pltpu.make_async_copy(h_hbm.at[:, pl.ds(j * 256, 256)], h_buf.at[:, pl.ds(j * 256, 256)], h_sem.at[j])

    barrier = pltpu.get_barrier_semaphore()
    partners = [*to_x[1:], *to_y[1:], *to_z[1:], to_core]
    for partner in partners:
        pl.semaphore_signal(barrier, inc=1, device_id=partner, device_id_type=MESH)
    for j in range(4):
        h_load(j).start()
    for k in range(8):
        for whose in range(2):
            for half in range(2):
                g_local(k, whose, half).start()

    live = live_ref[0, 0]

    def turn(j):
        h_load(j).wait()
        alive = lax.broadcasted_iota(I32, (TOK, 256), 0) < live
        block = jnp.where(alive, h_buf[:, pl.ds(j * 256, 256)].astype(F32), 0.0)
        ht[pl.ds(j * 256, 256), :] = block.T.astype(BF16)

    for j in range(4):
        turn(j)
    pl.semaphore_wait(barrier, len(partners))

    def rows_of(block, start, count=16):
        return pl.ds(pl.multiple_of(block * BLK + start, 16), count)

    def a_tile(k, tx, half, i):
        return s_buf[k, half, rows_of((i // 3) * 4 + tx, 16 * (i % 3)), :]

    def b_tile(k, ty, half, i):
        return s_buf[k, lax.div(ty, 2), rows_of(lax.rem(ty, 2) * 4 + 2 * half + i // 3, 48 + 16 * (i % 3)), :]

    def hop(stage, axis, k, d):
        src, dst, send, recv = ((m1s, m1r, one_s, one_r.at[k]), (m2s, m2r, two_s, two_r.at[k // 2]))[stage]
        to = (to_x, to_y)[axis][1 if d == 0 else 3]
        return remote(src.at[k, axis, d], dst.at[k, axis, d], send, recv, to)

    tiles = (a_tile, b_tile)
    here = (xs_at, ys_at)

    def first_hop(k):
        for axis in range(2):
            tile, me = tiles[axis], here[axis]
            for d in range(2):
                near, far = me[1 if d == 0 else 3], me[2]

                def load(i, d=d, near=near, far=far, tile=tile):
                    return tile(k, far, d, i) if i < 6 else tile(k, near, 1 - d, i - 6)

                send_codes(load, 12, m1s.at[k, axis, d])
                hop(0, axis, k, d).start()

    def second_hop(k):
        wait_for(m1r.at[k], one_r.at[k])
        for axis in range(2):
            tile, me = tiles[axis], here[axis]
            for d in range(2):
                near = me[1 if d == 0 else 3]
                message = m1r.at[k, axis, d]
                unit = unit_of(message)

                def load(i, d=d, near=near, message=message, unit=unit, tile=tile):
                    return tile(k, near, d, i) + decode(message, i, unit)

                send_codes(load, 6, m2s.at[k, axis, d])
                hop(1, axis, k, d).start()

    def p2(axis, g, j):
        to = (to_y, to_x)[axis][j]
        return remote(p2s.at[g, axis, j - 1], p2r.at[g, axis, j - 1], p2_s, p2_r.at[g], to)

    def second_stage(g):
        wait_for(m2r.at[pl.ds(2 * g, 2)], two_r.at[g])
        for axis in range(2):
            tile, me = tiles[axis], here[axis]
            for zi in range(2):
                k = 2 * g + zi
                for half in range(2):
                    far, near = m2r.at[k, axis, half], m1r.at[k, axis, 1 - half]
                    far_unit, near_unit = unit_of(far), unit_of(near)
                    for i in range(6):
                        total = tile(k, me[0], half, i) + decode(far, i, far_unit) + decode(near, i + 6, near_unit)
                        part[axis, 2 * half + i // 3, zi * 3 + i % 3] = total
            other = here[1 - axis]
            for j in range(1, 4):
                send_codes(lambda i, axis=axis, target=other[j]: part[axis, target, i], 6, p2s.at[g, axis, j - 1])
                p2(axis, g, j).start()
            for i in range(6):
                keep2[g, i // 3, axis * 3 + i % 3] = part[axis, other[0], i]

    def p3(g, zi):
        k = 2 * g + zi
        at = lax.rem(z + (3 - g if zi else 4 + g), NZ)
        return remote(p3s.at[k], p3r.at[k], p3_s, p3_r, (yh * 16 + at * 2 + core, local))

    def third_stage(g):
        wait_for(p2r.at[g], p2_r.at[g])
        for axis in range(2):
            units = [unit_of(p2r.at[g, axis, j]) for j in range(3)]
            for i in range(6):
                total = keep2[g, i // 3, axis * 3 + i % 3]
                for j in range(3):
                    total += decode(p2r.at[g, axis, j], i, units[j])
                keep2[g, i // 3, axis * 3 + i % 3] = total
        for zi in range(2):

            def out(zi=zi):
                send_codes(lambda i: keep2[g, zi, i], 6, p3s.at[2 * g + zi])
                p3(g, zi).start()

            if zi == 0:
                out()
            else:
                pl.when(g < GROUPS - 1)(out)

    def c_tile(k, half, i):
        return s_buf[k, half, rows_of(i // 2, 96 + 16 * (i % 2)), :]

    def c1(d, s, p):
        i = s - 1 + 4 * p
        return remote(c1s.at[i, d], c1r.at[i, d], c1_s, c1_r.at[i, d], to_z[1 if d == 0 else 7])

    def z_index(d, distance):
        return 0 if distance == 4 else 7 - 2 * distance + d

    def z_hop(d, s):
        for p in range(2 if s < 4 else 1):
            k, half = z_index(d, 5 - s - p), d if p == 0 else 1 - d
            if s > 1:
                c1(d, s - 1, p).wait_recv()
                message = c1r.at[s - 2 + 4 * p, d]
                unit = unit_of(message)

            def load(i):
                value = c_tile(k, half, i)
                return value + decode(message, i, unit) if s > 1 else value

            send_codes(load, 16, c1s.at[s - 1 + 4 * p, d])
            c1(d, s, p).start()

    def c2(j):
        return remote(c2s.at[j - 1], c2r.at[j - 1], c2_s, c2_r, to_x[j])

    def c3(j):
        return remote(c3s.at[j - 1], c3r.at[j - 1], c3_s, c3_r, to_y[j])

    def c_second():
        for d in range(2):
            c1(d, 4, 0).wait_recv()
            c1(d, 3, 1).wait_recv()
        for half in range(2):
            far, near = c1r.at[3, half], c1r.at[6, 1 - half]
            far_unit, near_unit = unit_of(far), unit_of(near)
            for i in range(16):
                block, t = i // 2, i % 2
                total = c_tile(7, half, i) + decode(far, i, far_unit) + decode(near, i, near_unit)
                rc[block % 4, half * 2 + block // 4, t] = total
        for j in range(1, 4):
            target = xs_at[j]
            send_codes(lambda i, target=target: rc[target, i // 2, i % 2], 8, c2s.at[j - 1])
            c2(j).start()

    def c_third():
        wait_for(c2r, c2_r)
        units = [unit_of(c2r.at[j]) for j in range(3)]
        for i in range(8):
            total = rc[x, i // 2, i % 2]
            for j in range(3):
                total += decode(c2r.at[j], i, units[j])
            kc[i // 2, i % 2] = total
        for j in range(1, 4):
            target = ys_at[j]
            send_codes(lambda i, target=target: kc[target, i], 2, c3s.at[j - 1])
            c3(j).start()

    def c_last():
        wait_for(c3r, c3_r)
        units = [unit_of(c3r.at[j]) for j in range(3)]
        for i in range(2):
            total = kc[y, i]
            for j in range(3):
                total += decode(c3r.at[j], i, units[j])
            grad[96 + 16 * i : 112 + 16 * i, :] = total

    def multiply(k):
        wait_for(gb.at[k], gl_sem.at[k])
        product = jnp.dot(ht[...], gb[k], preferred_element_type=F32)
        for half in range(2):
            s_buf[k, half] = product[:, half * BLK : half * BLK + BLK]
            xs[k, half] = product[:, (2 + half) * BLK : (3 + half) * BLK]
        swap(k).start()

    def add_core(k):
        swap(k).wait_recv()

        def add(block, carry):
            rows = rows_of(block, 0, BLK)
            for half in range(2):
                s_buf[k, half, rows, :] += xr[k, half, rows, :]
            return carry

        lax.fori_loop(0, 8, add, 0)

    def round_of(it, carry):
        pl.when(it < 8)(lambda: multiply(it))

        @pl.when((it >= 1) & (it < 9))
        def _():
            add_core(it - 1)
            first_hop(it - 1)

        for s, when in enumerate(Z_AT, 1):
            for d in range(2):
                pl.when(it == when[d])(functools.partial(z_hop, d, s))

        pl.when((it >= LAG[0]) & (it < LAG[0] + 8))(lambda: second_hop(it - LAG[0]))
        pl.when((it >= LAG[1]) & (it < LAG[1] + 7) & ((it - LAG[1]) % 2 == 0))(lambda: second_stage((it - LAG[1]) // 2))
        pl.when(it == C_AT[0])(c_second)
        pl.when(it == C_AT[1])(c_third)
        pl.when((it >= LAG[2]) & ((it - LAG[2]) % 2 == 0))(lambda: third_stage((it - LAG[2]) // 2))
        return carry

    lax.fori_loop(0, LAG[2] + 7, round_of, 0)
    wait_for(p3r, p3_r)
    units = [unit_of(p3r.at[k]) for k in range(7)]
    for i in range(6):
        total = keep2[GROUPS - 1, 1, i]
        for k in range(7):
            total += decode(p3r.at[k], i, units[k])
        grad[16 * i : 16 * i + 16, :] = total
    c_last()

    new_master, new_first, new_second = adamw(grad[...], master_ref[...], first_ref[...], second_ref[...])

    def w_at(dz=0, other=0):
        return w_buf.at[:, pl.ds(pl.multiple_of(z_nodes[other][dz] * BLK, BLK), BLK)]

    z_sends = ((0, 1, 0, BLK), (0, 7, 0, BLK), (0, 2, 0, BLK), (0, 6, 0, BLK), (6, 1, 0, BLK), (2, 7, 0, BLK), (6, 2, 0, 64), (2, 6, 64, 64))

    def w_z(i):
        block, to, start, count = z_sends[i]
        at = w_at(block).at[pl.ds(start, count)]
        return remote(at, at, wz_s, wz_r.at[min(i, 6)], to_z[to])

    def blocks(count):
        return w_buf.at[:, pl.ds(0, count * BLK)]

    def w_z_got(i):
        wait_for(blocks(1), wz_r.at[i])

    def w_y(j):
        at = w_at(-j % NZ)
        return remote(at, at, wy_s, wy_r.at[j], to_y[2])

    def w_c(j, other):
        at = w_at(-j % NZ, other)
        return remote(at, at, wc_s, wc_r, to_core)

    w_at()[...] = new_master.astype(BF16)

    def spread(j):
        w_y(j).start()
        w_c(j, 0).start()

    for i in (2, 3, 0, 1):
        w_z(i).start()
    spread(0)
    new_master_ref[...] = new_master
    new_first_ref[...] = new_first
    new_second_ref[...] = new_second
    w_z_got(2)
    w_z(4).start()
    w_z(6).start()
    w_z_got(3)
    w_z(5).start()
    w_z(7).start()
    for i, j in ((0, 1), (1, 7)):
        w_z_got(i)
        spread(j)
    spread(2)
    spread(6)
    for i, j in ((4, 3), (5, 5), (6, 4)):
        w_z_got(i)
        spread(j)
    for j in (0, 1, 7, 2, 6, 3, 5, 4):
        wait_for(blocks(1), wy_r.at[j])
        w_c(j, 1).start()
    wait_for(blocks(16), wc_r)
    w_ref[...] = w_buf[...]

    for ref, sem in (
        (xs, xs_sem), (m1s, one_s), (m2s, two_s), (p2s, p2_s), (p3s, p3_s), (c1s, c1_s), (c2s, c2_s), (c3s, c3_s),
        (blocks(7), wz_s), (blocks(8), wy_s), (blocks(16), wc_s),
    ):
        wait_for(ref, sem)


def body(hidden_acts, out_grad, live_counts, master, first, second):
    vmem, smem, anywhere = (pl.BlockSpec(memory_space=m) for m in (pltpu.VMEM, pltpu.SMEM, pl.ANY))
    dma = pltpu.SemaphoreType.DMA

    def tiles(*shape, kind=I16):
        return pltpu.VMEM((*shape, 16, BLK), kind)

    block = pltpu.VMEM((BLK, BLK), F32)
    results = pl.pallas_call(
        kernel,
        out_shape=(block, block, block, pltpu.VMEM((BLK, D), BF16)),
        in_specs=[anywhere, anywhere, smem, vmem, vmem, vmem],
        out_specs=(vmem, vmem, vmem, vmem),
        scratch_shapes=[
            pltpu.VMEM((TOK, FFW), BF16),
            pltpu.VMEM((FFW, TOK), BF16),
            pltpu.VMEM((8, TOK, 4 * BLK), BF16),
            pltpu.VMEM((8, 2, FFW, BLK), F32), pltpu.VMEM((8, 2, FFW, BLK), F32), pltpu.VMEM((8, 2, FFW, BLK), F32),
            tiles(8, 2, 2, 13), tiles(8, 2, 2, 13), tiles(8, 2, 2, 7), tiles(8, 2, 2, 7),
            tiles(2, 4, 6, kind=F32), tiles(4, 2, 6, kind=F32),
            tiles(4, 2, 3, 7), tiles(4, 2, 3, 7), tiles(7, 7), tiles(7, 7),
            tiles(7, 2, 17), tiles(7, 2, 17), tiles(4, 4, 2, kind=F32),
            tiles(3, 9), tiles(3, 9), tiles(4, 2, kind=F32), tiles(3, 3), tiles(3, 3),
            pltpu.VMEM((BLK, BLK), F32),
            pltpu.VMEM((BLK, D), BF16),
            dma((4,)), dma((8,)), dma(()), dma((8,)), dma(()), dma((8,)), dma(()), dma((4,)), dma(()), dma((4,)), dma(()), dma(()),
            dma(()), dma((7, 2)), dma(()), dma(()), dma(()), dma(()),
            dma(()), dma((7,)), dma(()), dma((8,)), dma(()), dma(()),
        ],
        compiler_params=pltpu.CompilerParams(
            collective_id=0, has_side_effects=True, vmem_limit_bytes=60 * 1024 * 1024
        ),
        cost_estimate=pl.CostEstimate(
            flops=2 * TOK * FFW * D, bytes_accessed=12 * 1024 * 1024, transcendentals=0
        ),
        name="grad_update",
    )(hidden_acts, out_grad, live_counts, master, first, second)
    return pl.pallas_call(
        hand_out,
        out_shape=[jax.ShapeDtypeStruct(r.shape, r.dtype) for r in results],
        in_specs=[vmem] * 4,
        out_specs=[anywhere] * 4,
        scratch_shapes=[dma((4,))],
        name="hand_out",
    )(*(pltpu.with_memory_space_constraint(r, pltpu.VMEM) for r in results))

def solution(mesh):
    in_specs = (
        P(("node", "local"), None),
        P(("node", "local"), None),
        P("node", "local"),
        P("local", "node"),
        P("local", "node"),
        P("local", "node"),
    )
    out_specs = (P("local", "node"), P("local", "node"), P("local", "node"), P("local", None))
    return jax.shard_map(body, mesh=mesh, in_specs=in_specs, out_specs=out_specs, check_vma=False)
```

```python
import functools

import jax
import jax.numpy as jnp
from jax import lax
from jax.experimental import pallas as pl
from jax.experimental.pallas import tpu as pltpu
from jax.sharding import PartitionSpec as P

ADAM_STEP = 10
MESH = pl.DeviceIdType.MESH
F32, BF16, I16, I32 = jnp.float32, jnp.bfloat16, jnp.int16, jnp.int32
NX, NY, NZ = 4, 4, 8
TOK, FFW, D = 1024, 1024, 4096
BLK = 128
GROUPS = 4
TOP = 32000.0
Z_AT = ((2, 3), (5, 6), (7, 8), (9, 9))
C_AT = (11, 13)
LAG = (4, 7, 9)
FAR = (4, 3, 5)


def send_codes(load, count, out):
    peak = functools.reduce(jnp.maximum, [jnp.abs(load(i)) for i in range(count)])
    power = jnp.ceil(jnp.log2(jnp.maximum(peak, 1e-30)) * 64.0)
    scale = jnp.exp2(power * (-1.0 / 64.0)) * TOP
    out[0] = power.astype(I32).astype(I16)
    for i in range(count):
        out[i + 1] = jnp.round(load(i) * scale).astype(I32).astype(I16)


def unit_of(message):
    return jnp.exp2(message[0].astype(I32).astype(F32) * (1.0 / 64.0)) * (1.0 / TOP)


def decode(message, i, unit):
    return message[i + 1].astype(I32).astype(F32) * unit


def adamw(grad, master, first, second):
    new_first = 0.9 * first + 0.1 * grad
    new_second = 0.95 * second + 0.05 * grad * grad
    update = (
        new_first
        / (1.0 - 0.9**ADAM_STEP)
        / (jnp.sqrt(new_second / (1.0 - 0.95**ADAM_STEP)) + 1e-08)
    )
    return master - 0.02 * (update + 0.1 * master), new_first, new_second


def hand_out(*refs):
    sources, targets, sem = refs[:4], refs[4:8], refs[8]
    copies = [pltpu.make_async_copy(a, b, sem.at[i]) for i, (a, b) in enumerate(zip(sources, targets))]
    for copy in copies:
        copy.start()
    for copy in copies:
        copy.wait()


def kernel(
    h_hbm, g_hbm, live_ref, master_ref, first_ref, second_ref,
    new_master_ref, new_first_ref, new_second_ref, w_ref,
    h_buf, ht, gb, theirs, xs, xr, s_buf, m1s, m1r, m2s, m2r, part, keep2, p2s, p2r, p3s, p3r,
    c1s, c1r, rc, c2s, c2r, kc, c3s, c3r, grad, w_buf,
    h_sem, gl_sem, xs_sem, xr_sem, one_s, one_r, two_s, two_r, p2_s, p2_r, p3_s, p3_r,
    c1_s, c1_r, c2_s, c2_r, c3_s, c3_r, wz_s, wz_r, wy_s, wy_r, wc_s, wc_r,
):
    node, local = lax.axis_index("node"), lax.axis_index("local")
    core, z, yh = lax.rem(node, 2), lax.rem(lax.div(node, 2), NZ), lax.div(node, 16)
    x, yl = lax.rem(local, 4), lax.div(local, 4)
    y = yh * 2 + yl

    xs_at = [lax.rem(x + i, NX) for i in range(NX)]
    ys_at = [lax.rem(y + i, NY) for i in range(NY)]
    zs_at = [lax.rem(z + i, NZ) for i in range(NZ)]
    to_x = [(node, yl * 4 + at) for at in xs_at]
    to_y = [(lax.div(at, 2) * 16 + lax.rem(node, 16), lax.rem(at, 2) * 4 + x) for at in ys_at]
    z_nodes = [[half * 16 + at * 2 + core for at in zs_at] for half in (yh, 1 - yh)]
    to_z = [(at, local) for at in z_nodes[0]]
    to_far = [(z_nodes[1][i], local) for i in FAR]
    to_core = (node + 1 - 2 * core, local)

    def remote(src, dst, send, recv, to):
        return pltpu.make_async_remote_copy(
            src_ref=src, dst_ref=dst, send_sem=send, recv_sem=recv, device_id=to, device_id_type=MESH
        )

    def cols(k, half, whose):
        away = 4 + k // 2 if k % 2 == 0 else 3 - k // 2
        block = half * 16 + zs_at[away] * 2 + (1 - core if whose else core)
        return pl.ds(pl.multiple_of(block * BLK, BLK), BLK)

    def g_local(k, whose, half):
        return pltpu.make_async_copy(
            g_hbm.at[:, cols(k, half, whose)],
            gb.at[k, :, pl.ds((2 * whose + half) * BLK, BLK)],
            gl_sem.at[k],
        )

    def swap(k, block):
        return remote(xs.at[k, block], xr.at[k, block], xs_sem, xr_sem.at[k], to_core)

    def wait_for(ref, sem):
        pltpu.make_async_copy(ref, ref, sem).wait()

    def h_load(j):
        return pltpu.make_async_copy(h_hbm.at[:, pl.ds(j * 256, 256)], h_buf.at[:, pl.ds(j * 256, 256)], h_sem.at[j])

    barrier = pltpu.get_barrier_semaphore()
    partners = [*to_x[1:], *to_y[1:], *to_z[1:], to_core, *to_far]
    for partner in partners:
        pl.semaphore_signal(barrier, inc=1, device_id=partner, device_id_type=MESH)
    for j in range(4):
        h_load(j).start()
    for k in range(8):
        for whose in range(2):
            for half in range(2):
                g_local(k, whose, half).start()

    live = live_ref[0, 0]

    def turn(j):
        h_load(j).wait()
        alive = lax.broadcasted_iota(I32, (TOK, 256), 0) < live
        block = jnp.where(alive, h_buf[:, pl.ds(j * 256, 256)].astype(F32), 0.0)
        ht[pl.ds(j * 256, 256), :] = block.T.astype(BF16)

    for j in range(4):
        turn(j)
    pl.semaphore_wait(barrier, len(partners))

    def rows_of(block, start, count=16):
        return pl.ds(pl.multiple_of(block * BLK + start, 16), count)

    def a_tile(k, tx, half, i):
        return s_buf[k, half, rows_of((i // 3) * 4 + tx, 16 * (i % 3)), :]

    def b_tile(k, ty, half, i):
        return s_buf[k, lax.div(ty, 2), rows_of(lax.rem(ty, 2) * 4 + 2 * half + i // 3, 48 + 16 * (i % 3)), :]

    def hop(stage, axis, k, d):
        src, dst, send, recv = ((m1s, m1r, one_s, one_r.at[k]), (m2s, m2r, two_s, two_r.at[k // 2]))[stage]
        to = (to_x, to_y)[axis][1 if d == 0 else 3]
        return remote(src.at[k, axis, d], dst.at[k, axis, d], send, recv, to)

    tiles = (a_tile, b_tile)
    here = (xs_at, ys_at)

    def first_hop(k):
        for axis in range(2):
            tile, me = tiles[axis], here[axis]
            for d in range(2):
                near, far = me[1 if d == 0 else 3], me[2]

                def load(i, d=d, near=near, far=far, tile=tile):
                    return tile(k, far, d, i) if i < 6 else tile(k, near, 1 - d, i - 6)

                send_codes(load, 12, m1s.at[k, axis, d])
                hop(0, axis, k, d).start()

    def second_hop(k):
        wait_for(m1r.at[k], one_r.at[k])
        for axis in range(2):
            tile, me = tiles[axis], here[axis]
            for d in range(2):
                near = me[1 if d == 0 else 3]
                message = m1r.at[k, axis, d]
                unit = unit_of(message)

                def load(i, d=d, near=near, message=message, unit=unit, tile=tile):
                    return tile(k, near, d, i) + decode(message, i, unit)

                send_codes(load, 6, m2s.at[k, axis, d])
                hop(1, axis, k, d).start()

    def p2(axis, g, j):
        to = (to_y, to_x)[axis][j]
        return remote(p2s.at[g, axis, j - 1], p2r.at[g, axis, j - 1], p2_s, p2_r.at[g], to)

    def second_stage(g):
        wait_for(m2r.at[pl.ds(2 * g, 2)], two_r.at[g])
        for axis in range(2):
            tile, me = tiles[axis], here[axis]
            for zi in range(2):
                k = 2 * g + zi
                for half in range(2):
                    far, near = m2r.at[k, axis, half], m1r.at[k, axis, 1 - half]
                    far_unit, near_unit = unit_of(far), unit_of(near)
                    for i in range(6):
                        total = tile(k, me[0], half, i) + decode(far, i, far_unit) + decode(near, i + 6, near_unit)
                        part[axis, 2 * half + i // 3, zi * 3 + i % 3] = total
            other = here[1 - axis]
            for j in range(1, 4):
                send_codes(lambda i, axis=axis, target=other[j]: part[axis, target, i], 6, p2s.at[g, axis, j - 1])
                p2(axis, g, j).start()
            for i in range(6):
                keep2[g, i // 3, axis * 3 + i % 3] = part[axis, other[0], i]

    def p3(g, zi):
        k = 2 * g + zi
        at = lax.rem(z + (3 - g if zi else 4 + g), NZ)
        return remote(p3s.at[k], p3r.at[k], p3_s, p3_r, (yh * 16 + at * 2 + core, local))

    def third_stage(g):
        wait_for(p2r.at[g], p2_r.at[g])
        for axis in range(2):
            units = [unit_of(p2r.at[g, axis, j]) for j in range(3)]
            for i in range(6):
                total = keep2[g, i // 3, axis * 3 + i % 3]
                for j in range(3):
                    total += decode(p2r.at[g, axis, j], i, units[j])
                keep2[g, i // 3, axis * 3 + i % 3] = total
        for zi in range(2):

            def out(zi=zi):
                send_codes(lambda i: keep2[g, zi, i], 6, p3s.at[2 * g + zi])
                p3(g, zi).start()

            if zi == 0:
                out()
            else:
                pl.when(g < GROUPS - 1)(out)

    def c_tile(k, half, i):
        return s_buf[k, half, rows_of(i // 2, 96 + 16 * (i % 2)), :]

    def c1(d, s, p):
        i = s - 1 + 4 * p
        return remote(c1s.at[i, d], c1r.at[i, d], c1_s, c1_r.at[i, d], to_z[1 if d == 0 else 7])

    def z_index(d, distance):
        return 0 if distance == 4 else 7 - 2 * distance + d

    def z_hop(d, s):
        for p in range(2 if s < 4 else 1):
            k, half = z_index(d, 5 - s - p), d if p == 0 else 1 - d
            if s > 1:
                c1(d, s - 1, p).wait_recv()
                message = c1r.at[s - 2 + 4 * p, d]
                unit = unit_of(message)

            def load(i):
                value = c_tile(k, half, i)
                return value + decode(message, i, unit) if s > 1 else value

            send_codes(load, 16, c1s.at[s - 1 + 4 * p, d])
            c1(d, s, p).start()

    def c2(j):
        return remote(c2s.at[j - 1], c2r.at[j - 1], c2_s, c2_r, to_x[j])

    def c3(j):
        return remote(c3s.at[j - 1], c3r.at[j - 1], c3_s, c3_r, to_y[j])

    def c_second():
        for d in range(2):
            c1(d, 4, 0).wait_recv()
            c1(d, 3, 1).wait_recv()
        for half in range(2):
            far, near = c1r.at[3, half], c1r.at[6, 1 - half]
            far_unit, near_unit = unit_of(far), unit_of(near)
            for i in range(16):
                block, t = i // 2, i % 2
                total = c_tile(7, half, i) + decode(far, i, far_unit) + decode(near, i, near_unit)
                rc[block % 4, half * 2 + block // 4, t] = total
        for j in range(1, 4):
            target = xs_at[j]
            send_codes(lambda i, target=target: rc[target, i // 2, i % 2], 8, c2s.at[j - 1])
            c2(j).start()

    def c_third():
        wait_for(c2r, c2_r)
        units = [unit_of(c2r.at[j]) for j in range(3)]
        for i in range(8):
            total = rc[x, i // 2, i % 2]
            for j in range(3):
                total += decode(c2r.at[j], i, units[j])
            kc[i // 2, i % 2] = total
        for j in range(1, 4):
            target = ys_at[j]
            send_codes(lambda i, target=target: kc[target, i], 2, c3s.at[j - 1])
            c3(j).start()

    def c_last():
        wait_for(c3r, c3_r)
        units = [unit_of(c3r.at[j]) for j in range(3)]
        for i in range(2):
            total = kc[y, i]
            for j in range(3):
                total += decode(c3r.at[j], i, units[j])
            grad[96 + 16 * i : 112 + 16 * i, :] = total

    def multiply(k):
        wait_for(gb.at[k], gl_sem.at[k])
        product = jnp.dot(ht[...], gb[k], preferred_element_type=F32)
        for half in range(2):
            s_buf[k, half] = product[:, half * BLK : half * BLK + BLK]
            theirs[half] = product[:, (2 + half) * BLK : (3 + half) * BLK]

        def quantize(block, carry):
            send_codes(lambda i: theirs[i // 8, rows_of(block, 16 * (i % 8)), :], 16, xs.at[k, block])
            swap(k, block).start()
            return carry

        lax.fori_loop(0, 8, quantize, 0)

    def add_core(k):
        wait_for(xr.at[k], xr_sem.at[k])

        def add(block, carry):
            message = xr.at[k, block]
            unit = unit_of(message)
            for i in range(16):
                s_buf[k, i // 8, rows_of(block, 16 * (i % 8)), :] += decode(message, i, unit)
            return carry

        lax.fori_loop(0, 8, add, 0)

    def round_of(it, carry):
        pl.when(it < 8)(lambda: multiply(it))

        @pl.when((it >= 1) & (it < 9))
        def _():
            add_core(it - 1)
            first_hop(it - 1)

        for s, when in enumerate(Z_AT, 1):
            for d in range(2):
                pl.when(it == when[d])(functools.partial(z_hop, d, s))

        pl.when((it >= LAG[0]) & (it < LAG[0] + 8))(lambda: second_hop(it - LAG[0]))
        pl.when((it >= LAG[1]) & (it < LAG[1] + 7) & ((it - LAG[1]) % 2 == 0))(lambda: second_stage((it - LAG[1]) // 2))
        pl.when(it == C_AT[0])(c_second)
        pl.when(it == C_AT[1])(c_third)
        pl.when((it >= LAG[2]) & ((it - LAG[2]) % 2 == 0))(lambda: third_stage((it - LAG[2]) // 2))
        return carry

    lax.fori_loop(0, LAG[2] + 7, round_of, 0)
    wait_for(p3r, p3_r)
    units = [unit_of(p3r.at[k]) for k in range(7)]
    for i in range(6):
        total = keep2[GROUPS - 1, 1, i]
        for k in range(7):
            total += decode(p3r.at[k], i, units[k])
        grad[16 * i : 16 * i + 16, :] = total
    c_last()

    new_master, new_first, new_second = adamw(grad[...], master_ref[...], first_ref[...], second_ref[...])

    def w_at(dz=0, other=0):
        return w_buf.at[:, pl.ds(pl.multiple_of(z_nodes[other][dz] * BLK, BLK), BLK)]

    z_sends = ((0, 1, 0, BLK), (0, 7, 0, BLK), (0, 2, 0, BLK), (0, 6, 0, BLK), (6, 1, 0, BLK), (2, 7, 0, BLK), (6, 2, 0, 64), (2, 6, 64, 64))

    def w_z(i):
        block, to, start, count = z_sends[i]
        at = w_at(block).at[pl.ds(start, count)]
        return remote(at, at, wz_s, wz_r.at[min(i, 6)], to_z[to])

    def blocks(count):
        return w_buf.at[:, pl.ds(0, count * BLK)]

    def w_z_got(i):
        wait_for(blocks(1), wz_r.at[i])

    def w_y(j):
        at = w_at(-j % NZ)
        return remote(at, at, wy_s, wy_r.at[j], to_y[2])

    def w_far(i):
        return remote(w_at(), w_at(), wy_s, wy_r.at[FAR[i]], to_far[i])

    def w_c(j, other):
        at = w_at(-j % NZ, other)
        return remote(at, at, wc_s, wc_r, to_core)

    w_at()[...] = new_master.astype(BF16)

    def spread(j):
        if j not in FAR:
            w_y(j).start()
        w_c(j, 0).start()

    for i in (2, 3):
        w_z(i).start()
    for i in range(3):
        w_far(i).start()
    for i in (0, 1):
        w_z(i).start()
    spread(0)
    new_master_ref[...] = new_master
    new_first_ref[...] = new_first
    new_second_ref[...] = new_second
    w_z_got(2)
    w_z(4).start()
    w_z(6).start()
    w_z_got(3)
    w_z(5).start()
    w_z(7).start()
    for i, j in ((0, 1), (1, 7)):
        w_z_got(i)
        spread(j)
    spread(2)
    spread(6)
    for i, j in ((4, 3), (5, 5), (6, 4)):
        w_z_got(i)
        spread(j)
    for j in (0, 1, 7, 2, 6, 3, 5, 4):
        wait_for(blocks(1), wy_r.at[j])
        w_c(j, 1).start()
    wait_for(blocks(16), wc_r)
    w_ref[...] = w_buf[...]

    for ref, sem in (
        (xs, xs_sem), (m1s, one_s), (m2s, two_s), (p2s, p2_s), (p3s, p3_s), (c1s, c1_s), (c2s, c2_s), (c3s, c3_s),
        (blocks(7), wz_s), (blocks(8), wy_s), (blocks(16), wc_s),
    ):
        wait_for(ref, sem)


def body(hidden_acts, out_grad, live_counts, master, first, second):
    vmem, smem, anywhere = (pl.BlockSpec(memory_space=m) for m in (pltpu.VMEM, pltpu.SMEM, pl.ANY))
    dma = pltpu.SemaphoreType.DMA

    def tiles(*shape, kind=I16):
        return pltpu.VMEM((*shape, 16, BLK), kind)

    block = pltpu.VMEM((BLK, BLK), F32)
    results = pl.pallas_call(
        kernel,
        out_shape=(block, block, block, pltpu.VMEM((BLK, D), BF16)),
        in_specs=[anywhere, anywhere, smem, vmem, vmem, vmem],
        out_specs=(vmem, vmem, vmem, vmem),
        scratch_shapes=[
            pltpu.VMEM((TOK, FFW), BF16),
            pltpu.VMEM((FFW, TOK), BF16),
            pltpu.VMEM((8, TOK, 4 * BLK), BF16),
            pltpu.VMEM((2, FFW, BLK), F32), tiles(8, 8, 17), tiles(8, 8, 17), pltpu.VMEM((8, 2, FFW, BLK), F32),
            tiles(8, 2, 2, 13), tiles(8, 2, 2, 13), tiles(8, 2, 2, 7), tiles(8, 2, 2, 7),
            tiles(2, 4, 6, kind=F32), tiles(4, 2, 6, kind=F32),
            tiles(4, 2, 3, 7), tiles(4, 2, 3, 7), tiles(7, 7), tiles(7, 7),
            tiles(7, 2, 17), tiles(7, 2, 17), tiles(4, 4, 2, kind=F32),
            tiles(3, 9), tiles(3, 9), tiles(4, 2, kind=F32), tiles(3, 3), tiles(3, 3),
            pltpu.VMEM((BLK, BLK), F32),
            pltpu.VMEM((BLK, D), BF16),
            dma((4,)), dma((8,)), dma(()), dma((8,)), dma(()), dma((8,)), dma(()), dma((4,)), dma(()), dma((4,)), dma(()), dma(()),
            dma(()), dma((7, 2)), dma(()), dma(()), dma(()), dma(()),
            dma(()), dma((7,)), dma(()), dma((8,)), dma(()), dma(()),
        ],
        compiler_params=pltpu.CompilerParams(
            collective_id=0, has_side_effects=True, vmem_limit_bytes=60 * 1024 * 1024
        ),
        cost_estimate=pl.CostEstimate(
            flops=2 * TOK * FFW * D, bytes_accessed=12 * 1024 * 1024, transcendentals=0
        ),
        name="grad_update",
    )(hidden_acts, out_grad, live_counts, master, first, second)
    return pl.pallas_call(
        hand_out,
        out_shape=[jax.ShapeDtypeStruct(r.shape, r.dtype) for r in results],
        in_specs=[vmem] * 4,
        out_specs=[anywhere] * 4,
        scratch_shapes=[dma((4,))],
        name="hand_out",
    )(*(pltpu.with_memory_space_constraint(r, pltpu.VMEM) for r in results))

def solution(mesh):
    in_specs = (
        P(("node", "local"), None),
        P(("node", "local"), None),
        P("node", "local"),
        P("local", "node"),
        P("local", "node"),
        P("local", "node"),
    )
    out_specs = (P("local", "node"), P("local", "node"), P("local", "node"), P("local", None))
    return jax.shard_map(body, mesh=mesh, in_specs=in_specs, out_specs=out_specs, check_vma=False)
```
